32 devices in a mesh: lat: 8 (over z, y), tok: 4 (over x, core).
Axes of the slice: x: 2, y: 2, z: 4, core: 2. Of those that a mesh axis runs over, the one named last changes fastest.
Arguments:
- inputs: bfloat16 [256, 3, 2304], P('lat', None, 'tok'), may hold values from -6 to 6
- targets: bfloat16 [256, 3, 2304], P('lat', None, 'tok'), may hold values from -6 to 6
- enc_weight: bfloat16 [3, 2304, 2048], P(None, 'tok', 'lat'), may hold values from -0.125 to 0.125
- enc_bias: float32 [3, 2048], P(None, 'lat'), may hold values from -3 to 3
- dec_weight: bfloat16 [6, 2048, 2304], P(None, 'lat', 'tok'), may hold values from -0.125 to 0.125
- counts: int32 [3, 8], P(None, 'lat'), may hold values from 32 to 256, as said below
Outputs:
- recon: bfloat16 [256, 3, 2304], P('lat', None, 'tok')
- dec_grad: bfloat16 [6, 2048, 2304], P(None, 'lat', 'tok')
- latent_grad: bfloat16 [256, 3, 2048], P('tok', None, 'lat')
The draws below stay inside these ranges and needn't reach their ends.
Inputs may be any that keep to these rules, and one draw needn't show every extreme that they name: Latents 0 to counts[l, t] - 1 of layer l's tile on index t of lat are live, the rest dead; in every layer some tile has all 256 live.
All inputs are finite; a program needn't handle non-finite values.
Results may differ from the reference program's by a relative error of at most 0.0054.
Values may be sent and summed in bfloat16 or wider, within the bound.
No kernel may reach another device: no remote copies, remote signals or barrier semaphores. Data moves between devices by JAX's collectives and lax.ppermute only.
A program may use at most 64 MiB of HBM per device.

```python
import jax
import jax.numpy as jnp

D = 2304
LAT_DEV = 256
L = 3
TOKENS = 256
LATENTS = 2048
BLOCKS = 6
N_LAT = 8


def draw_counts(key, part):
    first_key, second_key = jax.random.split(key, 2)
    spread = 7 * LAT_DEV // 8
    raw_values = jax.random.randint(first_key, (L, N_LAT), 0, spread + 1)
    skewed = LAT_DEV // 8 + raw_values * raw_values // spread
    full_tile = jax.random.randint(second_key, (L,), 0, N_LAT)
    chosen = jnp.arange(N_LAT, dtype=jnp.int32)[None, :] == full_tile[:, None]
    return jnp.where(chosen, LAT_DEV, skewed).astype(jnp.int32)


def steps_of(key, shape, cuts, smallest, largest):
    def one(axis_at, blocks):
        steps = jax.random.uniform(jax.random.fold_in(jax.random.fold_in(key, 6), axis_at), (blocks,), jnp.float32, smallest / len(cuts), largest / len(cuts))
        return jnp.repeat(jnp.exp(steps), shape[axis_at] // blocks).reshape((-1,) + (1,) * (len(shape) - axis_at - 1))

    factor_of = one(*cuts[0])
    for cut in cuts[1:]:
        factor_of = factor_of * one(*cut)
    return factor_of


def centred(key, shape, deviation, most, cuts=(), held_as=jnp.bfloat16):
    gain = steps_of(key, shape, cuts, -0.22, 0.18) if cuts else 1.0
    entries = jax.random.normal(key, shape, jnp.float32) * deviation * gain
    return jnp.minimum(jnp.maximum(entries, -most), most).astype(held_as)


def setup_inputs(seed: int = 0) -> dict:
    key_list = jax.random.split(jax.random.key(seed), 7)
    inputs = centred(key_list[0], (TOKENS, L, D), 1.0, 6.0, ((0, 8), (2, 4)))
    targets = centred(key_list[1], (TOKENS, L, D), 1.0, 6.0, ((0, 8), (2, 4)))
    enc_weight = centred(key_list[2], (L, D, LATENTS), D ** -0.5, 0.125, ((1, 4), (2, 8)))
    enc_bias = centred(key_list[3], (L, LATENTS), 0.5, 3.0, ((1, 8),), jnp.float32)
    dec_weight = centred(key_list[4], (BLOCKS, LATENTS, D), (LAT_DEV * N_LAT) ** -0.5, 0.125, ((1, 8), (2, 4)))
    counts = draw_counts(jax.random.fold_in(key_list[6], 71), 0)
    return dict(inputs=inputs, targets=targets, enc_weight=enc_weight, enc_bias=enc_bias, dec_weight=dec_weight, counts=counts)


def block_index(source, target):
    return source * L - source * (source - 1) // 2 + (target - source)


def reference(inputs, targets, enc_weight, enc_bias, dec_weight, counts):
    positions = jnp.arange(LAT_DEV * N_LAT, dtype=jnp.int32)
    live_mask = (positions % LAT_DEV)[None, :] < jnp.repeat(counts, LAT_DEV, axis=1)
    latents = []
    for source in range(L):
        preact = jnp.dot(inputs[:, source, :], enc_weight[source], preferred_element_type=jnp.float32)
        preact = preact + enc_bias[source][None, :]
        latents.append(jnp.where(live_mask[source][None, :], jnp.maximum(preact, 0.0), 0.0).astype(jnp.bfloat16))
    recons = []
    errors = []
    for target in range(L):
        summed = jnp.zeros((TOKENS, D), jnp.float32)
        for source in range(target + 1):
            summed = summed + jnp.dot(latents[source], dec_weight[block_index(source, target)], preferred_element_type=jnp.float32)
        recons.append(summed.astype(jnp.bfloat16))
        errors.append((summed - targets[:, target, :].astype(jnp.float32)).astype(jnp.bfloat16))
    grads = []
    for source in range(L):
        for target in range(source, L):
            grads.append(jnp.dot(latents[source].T, errors[target], preferred_element_type=jnp.float32).astype(jnp.bfloat16))
    latent_grads = []
    for source in range(L):
        summed = jnp.zeros((TOKENS, LAT_DEV * N_LAT), jnp.float32)
        for target in range(source, L):
            summed = summed + jnp.dot(errors[target], dec_weight[block_index(source, target)].T, preferred_element_type=jnp.float32)
        latent_grads.append(jnp.where(live_mask[source][None, :], summed, 0.0).astype(jnp.bfloat16))
    return jnp.stack(recons, axis=1), jnp.stack(grads, axis=0), jnp.stack(latent_grads, axis=1)
```

```python
import functools

import jax
import jax.numpy as jnp
from jax import lax
from jax.experimental import pallas as pl
from jax.experimental.pallas import tpu as pltpu
from jax.sharding import PartitionSpec as P

BF = jnp.bfloat16
F32 = jnp.float32
AXES = ("lat", "tok")


def block_index(source, target, layers):
    return source * layers - source * (source - 1) // 2 + (target - source)


def fused(body, outs, *args, scratch=(), scalars=1):
    specs = [pl.BlockSpec(memory_space=pltpu.SMEM)] * scalars
    specs += [pl.BlockSpec(memory_space=pltpu.VMEM)] * (len(args) - scalars)
    out_shape = [jax.ShapeDtypeStruct(s, d) for s, d in outs]
    return pl.pallas_call(
        body,
        out_shape=out_shape,
        in_specs=specs,
        out_specs=[pl.BlockSpec(memory_space=pltpu.VMEM)] * len(outs),
        scratch_shapes=[pltpu.VMEM(s, d) for s, d in scratch],
        compiler_params=pltpu.CompilerParams(vmem_limit_bytes=40 * 2**20),
    )(*args)


HOME, CORE, OFF = 0, 1, 2


def join_kernel(info, own, other, out):
    width = own.shape[2]

    @pl.when(info[CORE] == 0)
    def _():
        out[:, :, :width] = own[...]
        out[:, :, width:] = other[...]

    @pl.when(info[CORE] != 0)
    def _():
        out[:, :, :width] = other[...]
        out[:, :, width:] = own[...]


def stack_kernel(info, own, other, out):
    rows = own.shape[1]
    core = info[CORE]
    out[:, pl.ds(pl.multiple_of(core * rows, rows), rows), :] = own[...]
    out[:, pl.ds(pl.multiple_of((1 - core) * rows, rows), rows), :] = other[...]


def place(info, own, r1, r2, r3, r4, out):
    rows = own.shape[1]

    def at(i):
        return pl.ds(pl.multiple_of(info[OFF + i], rows), rows)

    @pl.when(info[HOME] != 0)
    def _():
        out[:, at(0), :] = own[...]
        out[:, at(1), :] = r2[...]

    @pl.when(info[HOME] == 0)
    def _():
        out[:, at(0), :] = r2[...]
        out[:, at(1), :] = r4[...]

    out[:, at(2), :] = r1[...]
    out[:, at(3), :] = r3[...]


def encode_kernel(info, own, r1, r2, r3, r4, weight, part, sent, held):
    place(info, own, r1, r2, r3, r4, held)
    for layer in range(part.shape[0]):
        value = jnp.dot(held[layer], weight[layer], preferred_element_type=F32)
        part[layer] = value
        sent[layer] = value.astype(BF)


def decode_kernel(info, counts, part, got, bias, weight, latents, q0, q1, q2, q3, recon):
    layers, half = part.shape[0], part.shape[1] // 2
    rows = q0.shape[1]
    width = part.shape[2]
    for layer in range(layers):
        live = lax.broadcasted_iota(jnp.int32, (half, width), 1) < counts[layer]
        for side in range(2):
            mine = pl.ds(side * half, half)
            theirs = pl.ds((1 - side) * half, half)
            pre = part[layer, mine, :] + got[layer, theirs, :].astype(F32) + bias[layer : layer + 1, :]
            latents[layer, mine, :] = jnp.where(live, jnp.maximum(pre, 0.0), 0.0).astype(BF)
    for target in range(layers):
        total = None
        for source in range(target + 1):
            value = lax.dot_general(
                latents[source],
                weight[block_index(source, target, layers)],
                (((1,), (1,)), ((), ())),
                preferred_element_type=F32,
            )
            total = value if total is None else total + value
        recon[...] = total

        def at(i):
            return recon[pl.ds(pl.multiple_of(info[OFF + i], rows), rows), :]

        q0[target] = at(0)
        q1[target] = at(1).astype(BF)
        q2[target] = at(2)
        q3[target] = at(3).astype(BF)


def add_keep_kernel(info, kept, got, total, sent):
    value = kept[...] + got[...].astype(F32)
    total[...] = value
    sent[...] = value.astype(BF)


def add_kernel(info, kept, got, sent):
    sent[...] = (kept[...] + got[...].astype(F32)).astype(BF)


def own_sum_kernel(info, kept, u0, u2, out):
    home = info[HOME] != 0
    out[...] = jnp.where(home, kept[...], u0[...].astype(F32)) + u2[...].astype(F32)


def error_kernel(info, mine, theirs, wanted, recon, errors):
    width = recon.shape[2]
    total = mine[...] + theirs[...]
    errors[...] = (total - wanted[...].astype(F32)).astype(BF)

    @pl.when(info[CORE] == 0)
    def _():
        recon[...] = total[:, :, :width].astype(BF)

    @pl.when(info[CORE] != 0)
    def _():
        recon[...] = total[:, :, width:].astype(BF)


def backward_kernel(info, own, r1, r2, r3, r4, weight, kept, sent, mine, other, held):
    place(info, own, r1, r2, r3, r4, held)
    layers, half = kept.shape[0], kept.shape[1]
    width = mine.shape[2]
    for source in range(layers):
        total = None
        for target in range(source, layers):
            value = jnp.dot(
                held[target], weight[block_index(source, target, layers)], preferred_element_type=F32
            )
            total = value if total is None else total + value
        kept[source] = total[:half]
        sent[source] = total[half:].astype(BF)

    @pl.when(info[CORE] == 0)
    def _():
        mine[...] = held[:, :, :width]
        other[...] = held[:, :, width:]

    @pl.when(info[CORE] != 0)
    def _():
        mine[...] = held[:, :, width:]
        other[...] = held[:, :, :width]


def weight_grad_kernel(info, errors, errors_got, latents, latents_got, out):
    layers = latents.shape[0]
    contract = (((0,), (0,)), ((), ()))
    for source in range(layers):
        for target in range(source, layers):
            total = lax.dot_general(errors[target], latents[source], contract, preferred_element_type=F32)
            total += lax.dot_general(
                errors_got[target], latents_got[source], contract, preferred_element_type=F32
            )
            out[block_index(source, target, layers)] = total.astype(BF)


def latent_grad_kernel(info, counts, kept, got, out):
    live_at = lax.broadcasted_iota(jnp.int32, kept.shape[1:], 1)
    for layer in range(kept.shape[0]):
        value = kept[layer] + got[layer].astype(F32)
        out[layer] = jnp.where(live_at < counts[layer], value, 0.0).astype(BF)


def make_paired(n_tok):
    places = [(z, y, x, c) for z in range(n_tok) for y in range(2) for x in range(n_tok // 2) for c in range(2)]

    def swap(value, where):
        pairs = []
        for i, (z, y, x, c) in enumerate(places):
            to = where(z, y, x, c, c == z % 2)
            if to is not None:
                pairs.append((i, places.index(to)))
        return lax.ppermute(value, AXES, pairs)

    def over_c(value):
        return swap(value, lambda z, y, x, c, home: (z, y, x, 1 - c))

    def over_x(value):
        return swap(value, lambda z, y, x, c, home: (z, y, 1 - x, c))

    def over_y(value):
        return swap(value, lambda z, y, x, c, home: (z, 1 - y, x, c))

    def over_y_away(value):
        return swap(value, lambda z, y, x, c, home: None if home else (z, 1 - y, x, c))

    def over_z2_z1(value):
        return swap(value, lambda z, y, x, c, home: (z ^ 2, y, x, c) if home else (z ^ 1, y, x, 1 - c))

    def over_y_z3(value):
        return swap(value, lambda z, y, x, c, home: (z, 1 - y, x, c) if home else (z ^ 3, y, x, 1 - c))

    def over_z3_away(value):
        return swap(value, lambda z, y, x, c, home: None if home else (z ^ 3, y, x, 1 - c))

    def gather(own):
        r1 = over_z2_z1(own)
        r2 = over_y_z3(own)
        return own, r1, r2, over_y(r1), over_y_away(r2)

    def local(inputs, targets, enc_weight, enc_bias, dec_weight, counts):
        rows, layers, width = inputs.shape
        latent_width = enc_weight.shape[2]
        both = 2 * width
        held = rows * 2 * n_tok // 2
        lat, tok = lax.axis_index("lat"), lax.axis_index("tok")
        z, y, x, c = lat // 2, lat % 2, tok // 2, tok % 2
        home = z % 2 == c
        near = jnp.where(home, z, z ^ 3)
        base = jnp.where(near // 2 == x, 0, held // 2)
        far = held // 2 - base
        info = jnp.stack(
            [home.astype(jnp.int32), c]
            + [base + rows * y, base + rows * (1 - y), far + rows * y, far + rows * (1 - y)]
        ).astype(jnp.int32)
        counts = counts[:, 0]

        own_in = jnp.swapaxes(inputs, 0, 1)
        own_want = jnp.swapaxes(targets, 0, 1)
        dec_t = jnp.swapaxes(dec_weight, 1, 2)
        (block,) = fused(join_kernel, [((layers, rows, both), BF)], info, own_in, over_c(own_in))
        arrived = gather(block)
        (wanted,) = fused(join_kernel, [((layers, rows, both), BF)], info, own_want, over_c(own_want))
        (enc_all,) = fused(stack_kernel, [((layers, both, latent_width), BF)], info, enc_weight, over_c(enc_weight))
        (dec_all,) = fused(stack_kernel, [((dec_t.shape[0], both, latent_width), BF)], info, dec_t, over_c(dec_t))

        tile = (layers, held, latent_width)
        rest = [((layers, held, both), BF)]
        part, sent = fused(encode_kernel, [(tile, F32), (tile, BF)], info, *arrived, enc_all, scratch=rest)
        piece = (layers, rows, both)
        latents, q0, q1, q2, q3 = fused(
            decode_kernel,
            [(tile, BF), (piece, F32), (piece, BF), (piece, F32), (piece, BF)],
            info,
            counts,
            part,
            over_x(sent),
            enc_bias,
            dec_all,
            scratch=[((held, both), F32)],
            scalars=2,
        )
        total, sent = fused(add_keep_kernel, [(piece, F32), (piece, BF)], info, q0, over_y(q1))
        u0 = over_z3_away(sent)
        (sent,) = fused(add_kernel, [(piece, BF)], info, q2, over_y(q3))
        u2 = over_z2_z1(sent)
        latents_got = over_c(latents)
        (mine,) = fused(own_sum_kernel, [(piece, F32)], info, total, u0, u2)
        recon, errors = fused(
            error_kernel, [((layers, rows, width), BF), (piece, BF)], info, mine, over_c(mine), wanted
        )
        arrived = gather(errors)
        quarter = (layers, held // 2, latent_width)
        wide = (layers, held, width)
        kept, sent, err_mine, err_other = fused(
            backward_kernel,
            [(quarter, F32), (quarter, BF), (wide, BF), (wide, BF)],
            info,
            *arrived,
            dec_all,
            scratch=rest,
        )
        got = over_x(sent)
        (grads,) = fused(
            weight_grad_kernel,
            [((dec_t.shape[0], width, latent_width), BF)],
            info,
            err_mine,
            over_c(err_other),
            latents,
            latents_got,
        )
        (latent_grad,) = fused(latent_grad_kernel, [(quarter, BF)], info, counts, kept, got, scalars=2)
        return jnp.swapaxes(recon, 0, 1), jnp.swapaxes(grads, 1, 2), jnp.swapaxes(latent_grad, 0, 1)

    return local


def general(inputs, targets, enc_weight, enc_bias, dec_weight, counts):
    layers = inputs.shape[1]
    width = enc_weight.shape[2]
    live = (lax.broadcasted_iota(jnp.int32, (layers, width), 1) < counts)[None]
    gathered = lax.all_gather(inputs, "lat", axis=0, tiled=True)
    part = jnp.einsum("tld,ldk->tlk", gathered, enc_weight, preferred_element_type=F32)
    preact = lax.psum(part, "tok") + enc_bias[None]
    latents = jnp.where(live, jnp.maximum(preact, 0.0), 0.0).astype(BF)
    recons = []
    for target in range(layers):
        recons.append(
            sum(
                jnp.dot(
                    latents[:, source],
                    dec_weight[block_index(source, target, layers)],
                    preferred_element_type=F32,
                )
                for source in range(target + 1)
            )
        )
    full = lax.psum_scatter(jnp.stack(recons, 1), "lat", scatter_dimension=0, tiled=True)
    own_errors = (full - targets.astype(F32)).astype(BF)
    errors = lax.all_gather(own_errors, "lat", axis=0, tiled=True)
    grads, sums = [], []
    for source in range(layers):
        total = 0.0
        for target in range(source, layers):
            weight = dec_weight[block_index(source, target, layers)]
            total = total + lax.dot_general(
                errors[:, target], weight, (((1,), (1,)), ((), ())), preferred_element_type=F32
            )
            grads.append(
                lax.dot_general(
                    latents[:, source],
                    errors[:, target],
                    (((0,), (0,)), ((), ())),
                    preferred_element_type=F32,
                ).astype(BF)
            )
        sums.append(total)
    latent_sum = lax.psum_scatter(jnp.stack(sums, 1), "tok", scatter_dimension=0, tiled=True)
    latent_grad = jnp.where(live, latent_sum, 0.0).astype(BF)
    return full.astype(BF), jnp.stack(grads, 0), latent_grad


def solution(mesh):
    n_lat, n_tok = mesh.shape["lat"], mesh.shape["tok"]
    in_specs = (
        P("lat", None, "tok"),
        P("lat", None, "tok"),
        P(None, "tok", "lat"),
        P(None, "lat"),
        P(None, "lat", "tok"),
        P(None, "lat"),
    )
    out_specs = (P("lat", None, "tok"), P(None, "lat", "tok"), P("tok", None, "lat"))
    paired = n_lat == 2 * n_tok and n_tok == 4
    local = make_paired(n_tok) if paired else general
    return jax.shard_map(local, mesh=mesh, in_specs=in_specs, out_specs=out_specs, check_vma=False)
```

```python
import functools

import jax
import jax.numpy as jnp
from jax import lax
from jax.experimental import pallas as pl
from jax.experimental.pallas import tpu as pltpu
from jax.sharding import PartitionSpec as P

BF = jnp.bfloat16
F32 = jnp.float32
AXES = ("lat", "tok")


def block_index(source, target, layers):
    return source * layers - source * (source - 1) // 2 + (target - source)


def fused(body, outs, *args, scratch=(), scalars=1):
    specs = [pl.BlockSpec(memory_space=pltpu.SMEM)] * scalars
    specs += [pl.BlockSpec(memory_space=pltpu.VMEM)] * (len(args) - scalars)
    out_shape = [jax.ShapeDtypeStruct(s, d) for s, d in outs]
    return pl.pallas_call(
        body,
        out_shape=out_shape,
        in_specs=specs,
        out_specs=[pl.BlockSpec(memory_space=pltpu.VMEM)] * len(outs),
        scratch_shapes=[pltpu.VMEM(s, d) for s, d in scratch],
        compiler_params=pltpu.CompilerParams(vmem_limit_bytes=40 * 2**20),
    )(*args)


HOME, CORE, NEAR = 0, 1, 2


def stack_kernel(info, own, other, out):
    rows = own.shape[1]
    core = info[CORE]
    out[:, pl.ds(pl.multiple_of(core * rows, rows), rows), :] = own[...]
    out[:, pl.ds(pl.multiple_of((1 - core) * rows, rows), rows), :] = other[...]


def place(info, own, r1, r2, r3, r4, out):
    rows = own.shape[1]

    @pl.when(info[HOME] != 0)
    def _():
        out[:, :rows, :] = own[...]
        out[:, rows : 2 * rows, :] = r2[...]

    @pl.when(info[HOME] == 0)
    def _():
        out[:, :rows, :] = r2[...]
        out[:, rows : 2 * rows, :] = r4[...]

    out[:, 2 * rows : 3 * rows, :] = r1[...]
    out[:, 3 * rows :, :] = r3[...]


def encode_kernel(info, own, r1, r2, r3, r4, weight, part, sent, held):
    place(info, own, r1, r2, r3, r4, held)
    for layer in range(part.shape[0]):
        value = jnp.dot(held[layer], weight[layer], preferred_element_type=F32)
        part[layer] = value
        sent[layer] = value.astype(BF)


def decode_kernel(counts, part, got, bias, weight, latents, kept0, kept1, sent0, sent1):
    kept, sent = (kept0, kept1), (sent0, sent1)
    layers, held, width = part.shape
    rows = kept0.shape[1]
    for layer in range(layers):
        live = lax.broadcasted_iota(jnp.int32, (held, width), 1) < counts[layer]
        pre = part[layer] + got[layer].astype(F32) + bias[layer : layer + 1, :]
        latents[layer] = jnp.where(live, jnp.maximum(pre, 0.0), 0.0).astype(BF)
    for target in range(layers):
        total = None
        for source in range(target + 1):
            value = lax.dot_general(
                latents[source],
                weight[block_index(source, target, layers)],
                (((1,), (1,)), ((), ())),
                preferred_element_type=F32,
            )
            total = value if total is None else total + value
        for i in range(2):
            kept[i][target] = total[2 * i * rows : (2 * i + 1) * rows]
            sent[i][target] = total[(2 * i + 1) * rows : (2 * i + 2) * rows].astype(BF)


def backward_kernel(info, own, r1, r2, r3, r4, weight, kept, sent, held):
    place(info, own, r1, r2, r3, r4, held)
    layers, half = kept.shape[0], kept.shape[1]
    for source in range(layers):
        total = None
        for target in range(source, layers):
            value = jnp.dot(
                held[target], weight[block_index(source, target, layers)], preferred_element_type=F32
            )
            total = value if total is None else total + value
        stays = info[NEAR] != 0
        kept[source] = jnp.where(stays, total[:half], total[half:])
        sent[source] = jnp.where(stays, total[half:], total[:half]).astype(BF)


def weight_grad_kernel(info, held, errors_got, latents, latents_got, out, own):
    layers = latents.shape[0]
    width = errors_got.shape[2]
    contract = (((0,), (0,)), ((), ()))

    @pl.when(info[CORE] == 0)
    def _():
        own[...] = held[:, :, :width]

    @pl.when(info[CORE] != 0)
    def _():
        own[...] = held[:, :, width:]

    for source in range(layers):
        values = jnp.concatenate([latents[source], latents_got[source]], 0)
        for target in range(source, layers):
            rows = jnp.concatenate([own[target], errors_got[target]], 0)
            total = lax.dot_general(rows, values, contract, preferred_element_type=F32)
            out[block_index(source, target, layers)] = total.astype(BF)


def make_paired(n_tok):
    places = [(z, y, x, c) for z in range(n_tok) for y in range(2) for x in range(n_tok // 2) for c in range(2)]

    def swap(value, where):
        pairs = []
        for i, (z, y, x, c) in enumerate(places):
            to = where(z, y, x, c, c == z % 2)
            if to is not None:
                pairs.append((i, places.index(to)))
        return lax.ppermute(value, AXES, pairs)

    def over_c(value):
        return swap(value, lambda z, y, x, c, home: (z, y, x, 1 - c))

    def over_x(value):
        return swap(value, lambda z, y, x, c, home: (z, y, 1 - x, c))

    def over_y(value):
        return swap(value, lambda z, y, x, c, home: (z, 1 - y, x, c))

    def over_y_away(value):
        return swap(value, lambda z, y, x, c, home: None if home else (z, 1 - y, x, c))

    def over_z2_z1(value):
        return swap(value, lambda z, y, x, c, home: (z ^ 2, y, x, c) if home else (z ^ 1, y, x, 1 - c))

    def over_y_z3(value):
        return swap(value, lambda z, y, x, c, home: (z, 1 - y, x, c) if home else (z ^ 3, y, x, 1 - c))

    def over_z3_away(value):
        return swap(value, lambda z, y, x, c, home: None if home else (z ^ 3, y, x, 1 - c))

    def gather(own):
        r1 = over_z2_z1(own)
        r2 = over_y_z3(own)
        return own, r1, r2, over_y(r1), over_y_away(r2)

    def local(inputs, targets, enc_weight, enc_bias, dec_weight, counts):
        rows, layers, width = inputs.shape
        latent_width = enc_weight.shape[2]
        both = 2 * width
        held = rows * n_tok
        lat, tok = lax.axis_index("lat"), lax.axis_index("tok")
        z, y, x, c = lat // 2, lat % 2, tok // 2, tok % 2
        home = z % 2 == c
        near = jnp.where(home, z, z ^ 3) // 2 == x
        info = jnp.stack([home, c, near]).astype(jnp.int32)
        dec_t = jnp.swapaxes(dec_weight, 1, 2)
        blocks = dec_t.shape[0]
        own_in, own_want = jnp.swapaxes(inputs, 0, 1), jnp.swapaxes(targets, 0, 1)

        def spread(own, first):
            rest = jnp.zeros_like(own)
            return jnp.where(first, jnp.concatenate([own, rest], 2), jnp.concatenate([rest, own], 2))

        def join(own, other):
            own = lax.optimization_barrier(spread(own, c == 0))
            left = lax.broadcasted_iota(jnp.int32, own.shape, 2) < width
            return jnp.where(left == (c == 0), own, spread(other, c != 0))

        block = join(own_in, over_c(own_in))
        block, enc_weight, dec_t, own_want = lax.optimization_barrier((block, enc_weight, dec_t, own_want))
        arrived = gather(block)
        (enc_all,) = fused(stack_kernel, [((layers, both, latent_width), BF)], info, enc_weight, over_c(enc_weight))
        (dec_all,) = fused(stack_kernel, [((blocks, both, latent_width), BF)], info, dec_t, over_c(dec_t))
        wanted = join(own_want, over_c(own_want))

        tile = (layers, held, latent_width)
        part, sent = fused(
            encode_kernel,
            [(tile, F32), (tile, BF)],
            info,
            *arrived,
            enc_all,
            scratch=[((layers, held, both), BF)],
        )
        piece = (layers, rows, both)
        latents, q0, q2, q1, q3 = fused(
            decode_kernel,
            [(tile, BF), (piece, F32), (piece, F32), (piece, BF), (piece, BF)],
            counts[:, 0],
            part,
            over_x(sent),
            enc_bias,
            dec_all,
        )
        q1, q3 = over_y(q1), over_y(q3)
        total = q0 + q1.astype(F32)
        u0 = over_z3_away(total.astype(BF))
        u2 = over_z2_z1((q2 + q3.astype(F32)).astype(BF))
        mine = jnp.where(home, total, u0.astype(F32)) + u2.astype(F32)
        full = mine + over_c(mine)
        errors = (full - wanted.astype(F32)).astype(BF)
        recon = jnp.where(c == 0, full[:, :, :width], full[:, :, width:]).astype(BF)
        arrived = gather(errors)
        latents_got = over_c(latents)
        arrived, recon, latents_got = lax.optimization_barrier((arrived, recon, latents_got))
        narrow = (layers, held // 2, latent_width)
        kept, sent, all_errors = fused(
            backward_kernel,
            [(narrow, F32), (narrow, BF), ((layers, held, both), BF)],
            info,
            *arrived,
            dec_all,
        )
        got = over_x(sent)
        other = jnp.where(c == 0, all_errors[:, :, width:], all_errors[:, :, :width])
        (grads,) = fused(
            weight_grad_kernel,
            [((blocks, width, latent_width), BF)],
            info,
            all_errors,
            over_c(other),
            latents,
            latents_got,
            scratch=[((layers, held, width), BF)],
        )
        got, grads = lax.optimization_barrier((got, grads))
        total = kept + got.astype(F32)
        flipped = jnp.concatenate([total[:, rows:], total[:, :rows]], 1)
        live = (lax.broadcasted_iota(jnp.int32, (layers, latent_width), 1) < counts)[:, None, :]
        latent_grad = jnp.where(live, jnp.where(y == 0, total, flipped), 0.0).astype(BF)
        return jnp.swapaxes(recon, 0, 1), jnp.swapaxes(grads, 1, 2), jnp.swapaxes(latent_grad, 0, 1)

    return local


def general(inputs, targets, enc_weight, enc_bias, dec_weight, counts):
    layers = inputs.shape[1]
    width = enc_weight.shape[2]
    live = (lax.broadcasted_iota(jnp.int32, (layers, width), 1) < counts)[None]
    gathered = lax.all_gather(inputs, "lat", axis=0, tiled=True)
    part = jnp.einsum("tld,ldk->tlk", gathered, enc_weight, preferred_element_type=F32)
    preact = lax.psum(part, "tok") + enc_bias[None]
    latents = jnp.where(live, jnp.maximum(preact, 0.0), 0.0).astype(BF)
    recons = []
    for target in range(layers):
        recons.append(
            sum(
                jnp.dot(
                    latents[:, source],
                    dec_weight[block_index(source, target, layers)],
                    preferred_element_type=F32,
                )
                for source in range(target + 1)
            )
        )
    full = lax.psum_scatter(jnp.stack(recons, 1), "lat", scatter_dimension=0, tiled=True)
    own_errors = (full - targets.astype(F32)).astype(BF)
    errors = lax.all_gather(own_errors, "lat", axis=0, tiled=True)
    grads, sums = [], []
    for source in range(layers):
        total = 0.0
        for target in range(source, layers):
            weight = dec_weight[block_index(source, target, layers)]
            total = total + lax.dot_general(
                errors[:, target], weight, (((1,), (1,)), ((), ())), preferred_element_type=F32
            )
            grads.append(
                lax.dot_general(
                    latents[:, source],
                    errors[:, target],
                    (((0,), (0,)), ((), ())),
                    preferred_element_type=F32,
                ).astype(BF)
            )
        sums.append(total)
    latent_sum = lax.psum_scatter(jnp.stack(sums, 1), "tok", scatter_dimension=0, tiled=True)
    latent_grad = jnp.where(live, latent_sum, 0.0).astype(BF)
    return full.astype(BF), jnp.stack(grads, 0), latent_grad


def solution(mesh):
    n_lat, n_tok = mesh.shape["lat"], mesh.shape["tok"]
    in_specs = (
        P("lat", None, "tok"),
        P("lat", None, "tok"),
        P(None, "tok", "lat"),
        P(None, "lat"),
        P(None, "lat", "tok"),
        P(None, "lat"),
    )
    out_specs = (P("lat", None, "tok"), P(None, "lat", "tok"), P("tok", None, "lat"))
    paired = n_lat == 2 * n_tok and n_tok == 4
    local = make_paired(n_tok) if paired else general
    return jax.shard_map(local, mesh=mesh, in_specs=in_specs, out_specs=out_specs, check_vma=False)
```

```python
import functools

import jax
import jax.numpy as jnp
from jax import lax
from jax.experimental import pallas as pl
from jax.experimental.pallas import tpu as pltpu
from jax.sharding import PartitionSpec as P

BF = jnp.bfloat16
F32 = jnp.float32
AXES = ("lat", "tok")


def block_index(source, target, layers):
    return source * layers - source * (source - 1) // 2 + (target - source)


def fused(body, outs, *args, scratch=(), scalars=1):
    specs = [pl.BlockSpec(memory_space=pltpu.SMEM)] * scalars
    specs += [pl.BlockSpec(memory_space=pltpu.VMEM)] * (len(args) - scalars)
    out_shape = [jax.ShapeDtypeStruct(s, d) for s, d in outs]
    return pl.pallas_call(
        body,
        out_shape=out_shape,
        in_specs=specs,
        out_specs=[pl.BlockSpec(memory_space=pltpu.VMEM)] * len(outs),
        scratch_shapes=[pltpu.VMEM(s, d) for s, d in scratch],
        compiler_params=pltpu.CompilerParams(vmem_limit_bytes=40 * 2**20),
    )(*args)


HOME, CORE, NEAR = 0, 1, 2


def stack_kernel(info, own, other, out):
    rows = own.shape[1]
    core = info[CORE]
    out[:, pl.ds(pl.multiple_of(core * rows, rows), rows), :] = own[...]
    out[:, pl.ds(pl.multiple_of((1 - core) * rows, rows), rows), :] = other[...]


def place(info, own, beside, third, fourth, r1, r3, out):
    rows = own.shape[1]

    @pl.when(info[HOME] != 0)
    def _():
        out[:, :rows, :] = own[...]
        out[:, rows : 2 * rows, :] = beside[...]

    @pl.when(info[HOME] == 0)
    def _():
        out[:, :rows, :] = third[...]
        out[:, rows : 2 * rows, :] = fourth[...]

    out[:, 2 * rows : 3 * rows, :] = r1[...]
    out[:, 3 * rows :, :] = r3[...]


def encode_kernel(info, own, beside, third, fourth, r1, r3, weight, part, sent, held):
    place(info, own, beside, third, fourth, r1, r3, held)
    for layer in range(part.shape[0]):
        value = jnp.dot(held[layer], weight[layer], preferred_element_type=F32)
        part[layer] = value
        sent[layer] = value.astype(BF)


def decode_kernel(counts, part, got, bias, weight, latents, kept0, kept1, sent0, sent1):
    kept, sent = (kept0, kept1), (sent0, sent1)
    layers, held, width = part.shape
    rows = kept0.shape[1]
    for layer in range(layers):
        live = lax.broadcasted_iota(jnp.int32, (held, width), 1) < counts[layer]
        pre = part[layer] + got[layer].astype(F32) + bias[layer : layer + 1, :]
        latents[layer] = jnp.where(live, jnp.maximum(pre, 0.0), 0.0).astype(BF)
    for target in range(layers):
        total = None
        for source in range(target + 1):
            value = lax.dot_general(
                latents[source],
                weight[block_index(source, target, layers)],
                (((1,), (1,)), ((), ())),
                preferred_element_type=F32,
            )
            total = value if total is None else total + value
        for i in range(2):
            kept[i][target] = total[2 * i * rows : (2 * i + 1) * rows]
            sent[i][target] = total[(2 * i + 1) * rows : (2 * i + 2) * rows].astype(BF)


def backward_kernel(info, own, beside, third, fourth, r1, r3, weight, kept, sent, held):
    place(info, own, beside, third, fourth, r1, r3, held)
    layers, half = kept.shape[0], kept.shape[1]
    for source in range(layers):
        total = None
        for target in range(source, layers):
            value = jnp.dot(
                held[target], weight[block_index(source, target, layers)], preferred_element_type=F32
            )
            total = value if total is None else total + value
        stays = info[NEAR] != 0
        kept[source] = jnp.where(stays, total[:half], total[half:])
        sent[source] = jnp.where(stays, total[half:], total[:half]).astype(BF)


def weight_grad_kernel(info, held, errors_got, latents, latents_got, out, own):
    layers = latents.shape[0]
    width = errors_got.shape[2]
    contract = (((0,), (0,)), ((), ()))

    @pl.when(info[CORE] == 0)
    def _():
        own[...] = held[:, :, :width]

    @pl.when(info[CORE] != 0)
    def _():
        own[...] = held[:, :, width:]

    for source in range(layers):
        values = jnp.concatenate([latents[source], latents_got[source]], 0)
        for target in range(source, layers):
            rows = jnp.concatenate([own[target], errors_got[target]], 0)
            total = lax.dot_general(rows, values, contract, preferred_element_type=F32)
            out[block_index(source, target, layers)] = total.astype(BF)


def make_paired(n_tok):
    places = [(z, y, x, c) for z in range(n_tok) for y in range(2) for x in range(n_tok // 2) for c in range(2)]

    def swap(value, where):
        pairs = []
        for i, (z, y, x, c) in enumerate(places):
            to = where(z, y, x, c, c == z % 2)
            if to is not None:
                pairs.append((i, places.index(to)))
        return lax.ppermute(value, AXES, pairs)

    def over_c(value):
        return swap(value, lambda z, y, x, c, home: (z, y, x, 1 - c))

    def over_x(value):
        return swap(value, lambda z, y, x, c, home: (z, y, 1 - x, c))

    def over_y(value):
        return swap(value, lambda z, y, x, c, home: (z, 1 - y, x, c))

    def over_z2_z1(value):
        return swap(value, lambda z, y, x, c, home: (z ^ 2, y, x, c) if home else (z ^ 1, y, x, 1 - c))


    def away_over_y(value):
        return swap(value, lambda z, y, x, c, home: (z ^ 1, y, x, 1 - c) if home else (z, 1 - y, x, c))

    def to_home_over_y(value):
        return swap(value, lambda z, y, x, c, home: (z, y if home else 1 - y, x, 1 - c))

    def to_away_over_z1(value):
        return swap(value, lambda z, y, x, c, home: (z ^ 1, y, x, c) if home else (z, y, x, 1 - c))

    def away_over_z3(value):
        return swap(value, lambda z, y, x, c, home: (z, 1 - y, x, c) if home else (z ^ 3, y, x, 1 - c))

    def gather(own):
        r1 = over_z2_z1(own)
        beside = to_home_over_y(own)
        third = to_away_over_z1(r1)
        r3 = over_y(r1)
        third, beside = lax.optimization_barrier((third, beside))
        return own, beside, third, away_over_y(third), r1, r3

    def reduce(q0, q1, q2, q3, home):
        near = q0 + over_y(q1).astype(F32)
        third = away_over_z3(near.astype(BF))
        got = over_z2_z1((q2 + over_y(q3).astype(F32)).astype(BF))
        return jnp.where(home, near, third.astype(F32)) + got.astype(F32)

    def local(inputs, targets, enc_weight, enc_bias, dec_weight, counts):
        rows, layers, width = inputs.shape
        latent_width = enc_weight.shape[2]
        both = 2 * width
        held = rows * n_tok
        lat, tok = lax.axis_index("lat"), lax.axis_index("tok")
        z, y, x, c = lat // 2, lat % 2, tok // 2, tok % 2
        home = z % 2 == c
        near = jnp.where(home, z, z ^ 3) // 2 == x
        info = jnp.stack([home, c, near]).astype(jnp.int32)
        dec_t = jnp.swapaxes(dec_weight, 1, 2)
        blocks = dec_t.shape[0]
        own_in, own_want = jnp.swapaxes(inputs, 0, 1), jnp.swapaxes(targets, 0, 1)

        def spread(own, first):
            rest = jnp.zeros_like(own)
            return jnp.where(first, jnp.concatenate([own, rest], 2), jnp.concatenate([rest, own], 2))

        def join(own, other):
            own = lax.optimization_barrier(spread(own, c == 0))
            left = lax.broadcasted_iota(jnp.int32, own.shape, 2) < width
            return jnp.where(left == (c == 0), own, spread(other, c != 0))

        block = join(own_in, over_c(own_in))
        block, enc_weight, dec_t, own_want = lax.optimization_barrier((block, enc_weight, dec_t, own_want))
        arrived = gather(block)
        (enc_all,) = fused(stack_kernel, [((layers, both, latent_width), BF)], info, enc_weight, over_c(enc_weight))
        (dec_all,) = fused(stack_kernel, [((blocks, both, latent_width), BF)], info, dec_t, over_c(dec_t))
        wanted = join(own_want, over_c(own_want))

        tile = (layers, held, latent_width)
        part, sent = fused(
            encode_kernel,
            [(tile, F32), (tile, BF)],
            info,
            *arrived,
            enc_all,
            scratch=[((layers, held, both), BF)],
        )
        piece = (layers, rows, both)
        latents, q0, q2, q1, q3 = fused(
            decode_kernel,
            [(tile, BF), (piece, F32), (piece, F32), (piece, BF), (piece, BF)],
            counts[:, 0],
            part,
            over_x(sent),
            enc_bias,
            dec_all,
        )
        mine = reduce(q0, q1, q2, q3, home)
        full = mine + over_c(mine)
        errors = (full - wanted.astype(F32)).astype(BF)
        recon = jnp.where(c == 0, full[:, :, :width], full[:, :, width:]).astype(BF)
        arrived = gather(errors)
        latents_got = over_c(latents)
        arrived, recon, latents_got = lax.optimization_barrier((arrived, recon, latents_got))
        narrow = (layers, held // 2, latent_width)
        kept, sent, all_errors = fused(
            backward_kernel,
            [(narrow, F32), (narrow, BF), ((layers, held, both), BF)],
            info,
            *arrived,
            dec_all,
        )
        got = over_x(sent)
        other = jnp.where(c == 0, all_errors[:, :, width:], all_errors[:, :, :width])
        (grads,) = fused(
            weight_grad_kernel,
            [((blocks, width, latent_width), BF)],
            info,
            all_errors,
            over_c(other),
            latents,
            latents_got,
            scratch=[((layers, held, width), BF)],
        )
        got, grads = lax.optimization_barrier((got, grads))
        total = kept + got.astype(F32)
        flipped = jnp.concatenate([total[:, rows:], total[:, :rows]], 1)
        live = (lax.broadcasted_iota(jnp.int32, (layers, latent_width), 1) < counts)[:, None, :]
        latent_grad = jnp.where(live, jnp.where(y == 0, total, flipped), 0.0).astype(BF)
        return jnp.swapaxes(recon, 0, 1), jnp.swapaxes(grads, 1, 2), jnp.swapaxes(latent_grad, 0, 1)

    return local


def general(inputs, targets, enc_weight, enc_bias, dec_weight, counts):
    layers = inputs.shape[1]
    width = enc_weight.shape[2]
    live = (lax.broadcasted_iota(jnp.int32, (layers, width), 1) < counts)[None]
    gathered = lax.all_gather(inputs, "lat", axis=0, tiled=True)
    part = jnp.einsum("tld,ldk->tlk", gathered, enc_weight, preferred_element_type=F32)
    preact = lax.psum(part, "tok") + enc_bias[None]
    latents = jnp.where(live, jnp.maximum(preact, 0.0), 0.0).astype(BF)
    recons = []
    for target in range(layers):
        recons.append(
            sum(
                jnp.dot(
                    latents[:, source],
                    dec_weight[block_index(source, target, layers)],
                    preferred_element_type=F32,
                )
                for source in range(target + 1)
            )
        )
    full = lax.psum_scatter(jnp.stack(recons, 1), "lat", scatter_dimension=0, tiled=True)
    own_errors = (full - targets.astype(F32)).astype(BF)
    errors = lax.all_gather(own_errors, "lat", axis=0, tiled=True)
    grads, sums = [], []
    for source in range(layers):
        total = 0.0
        for target in range(source, layers):
            weight = dec_weight[block_index(source, target, layers)]
            total = total + lax.dot_general(
                errors[:, target], weight, (((1,), (1,)), ((), ())), preferred_element_type=F32
            )
            grads.append(
                lax.dot_general(
                    latents[:, source],
                    errors[:, target],
                    (((0,), (0,)), ((), ())),
                    preferred_element_type=F32,
                ).astype(BF)
            )
        sums.append(total)
    latent_sum = lax.psum_scatter(jnp.stack(sums, 1), "tok", scatter_dimension=0, tiled=True)
    latent_grad = jnp.where(live, latent_sum, 0.0).astype(BF)
    return full.astype(BF), jnp.stack(grads, 0), latent_grad


def solution(mesh):
    n_lat, n_tok = mesh.shape["lat"], mesh.shape["tok"]
    in_specs = (
        P("lat", None, "tok"),
        P("lat", None, "tok"),
        P(None, "tok", "lat"),
        P(None, "lat"),
        P(None, "lat", "tok"),
        P(None, "lat"),
    )
    out_specs = (P("lat", None, "tok"), P(None, "lat", "tok"), P("tok", None, "lat"))
    paired = n_lat == 2 * n_tok and n_tok == 4
    local = make_paired(n_tok) if paired else general
    return jax.shard_map(local, mesh=mesh, in_specs=in_specs, out_specs=out_specs, check_vma=False)
```

```python
import functools

import jax
import jax.numpy as jnp
from jax import lax
from jax.experimental import pallas as pl
from jax.experimental.pallas import tpu as pltpu
from jax.sharding import PartitionSpec as P

BF = jnp.bfloat16
F32 = jnp.float32
AXES = ("lat", "tok")


def block_index(source, target, layers):
    return source * layers - source * (source - 1) // 2 + (target - source)


def fused(body, outs, *args, scratch=(), scalars=1):
    specs = [pl.BlockSpec(memory_space=pltpu.SMEM)] * scalars
    specs += [pl.BlockSpec(memory_space=pltpu.VMEM)] * (len(args) - scalars)
    out_shape = [jax.ShapeDtypeStruct(s, d) for s, d in outs]
    return pl.pallas_call(
        body,
        out_shape=out_shape,
        in_specs=specs,
        out_specs=[pl.BlockSpec(memory_space=pltpu.VMEM)] * len(outs),
        scratch_shapes=[pltpu.VMEM(s, d) for s, d in scratch],
        compiler_params=pltpu.CompilerParams(vmem_limit_bytes=40 * 2**20),
    )(*args)


HOME, CORE, NEAR = 0, 1, 2


def stack_kernel(info, own, other, out):
    rows = own.shape[1]
    core = info[CORE]
    out[:, pl.ds(pl.multiple_of(core * rows, rows), rows), :] = own[...]
    out[:, pl.ds(pl.multiple_of((1 - core) * rows, rows), rows), :] = other[...]


def place(info, own, beside, third, fourth, r1, r3, out):
    rows = own.shape[1]

    @pl.when(info[HOME] != 0)
    def _():
        out[:, :rows, :] = own[...]
        out[:, rows : 2 * rows, :] = beside[...]

    @pl.when(info[HOME] == 0)
    def _():
        out[:, :rows, :] = third[...]
        out[:, rows : 2 * rows, :] = fourth[...]

    out[:, 2 * rows : 3 * rows, :] = r1[...]
    out[:, 3 * rows :, :] = r3[...]


def encode_kernel(lo, info, own, beside, third, fourth, r1, r3, weight, part, sent, held):
    hi = lo + part.shape[0]
    blocks = [ref.at[lo:hi] for ref in (own, beside, third, fourth, r1, r3)]
    place(info, *blocks, held)
    for layer in range(lo, hi):
        value = jnp.dot(held[layer - lo], weight[layer], preferred_element_type=F32)
        part[layer - lo] = value
        sent[layer - lo] = value.astype(BF)


def decode_kernel(lo, layers, counts, part, got, bias, weight, *refs):
    before, after = refs[:-5], refs[-5:]
    for old, new in zip(before, after):
        new[:lo] = old[...]
    latents, kept0, kept1, sent0, sent1 = after
    kept, sent = (kept0, kept1), (sent0, sent1)
    held, width = part.shape[1:]
    rows = kept0.shape[1]
    for layer in range(lo, lo + part.shape[0]):
        live = lax.broadcasted_iota(jnp.int32, (held, width), 1) < counts[layer]
        pre = part[layer - lo] + got[layer - lo].astype(F32) + bias[layer : layer + 1, :]
        latents[layer] = jnp.where(live, jnp.maximum(pre, 0.0), 0.0).astype(BF)
    for target in range(lo, lo + part.shape[0]):
        total = None
        for source in range(target + 1):
            value = lax.dot_general(
                latents[source],
                weight[block_index(source, target, layers)],
                (((1,), (1,)), ((), ())),
                preferred_element_type=F32,
            )
            total = value if total is None else total + value
        for i in range(2):
            kept[i][target] = total[2 * i * rows : (2 * i + 1) * rows]
            sent[i][target] = total[(2 * i + 1) * rows : (2 * i + 2) * rows].astype(BF)


def backward_kernel(info, own, beside, third, fourth, r1, r3, weight, kept, sent, held):
    place(info, own, beside, third, fourth, r1, r3, held)
    layers, half = kept.shape[0], kept.shape[1]
    for source in range(layers):
        total = None
        for target in range(source, layers):
            value = jnp.dot(
                held[target], weight[block_index(source, target, layers)], preferred_element_type=F32
            )
            total = value if total is None else total + value
        stays = info[NEAR] != 0
        kept[source] = jnp.where(stays, total[:half], total[half:])
        sent[source] = jnp.where(stays, total[half:], total[:half]).astype(BF)


def weight_grad_kernel(info, held, errors_got, latents, latents_got, out, own):
    layers = latents.shape[0]
    width = errors_got.shape[2]
    contract = (((0,), (0,)), ((), ()))

    @pl.when(info[CORE] == 0)
    def _():
        own[...] = held[:, :, :width]

    @pl.when(info[CORE] != 0)
    def _():
        own[...] = held[:, :, width:]

    for source in range(layers):
        values = jnp.concatenate([latents[source], latents_got[source]], 0)
        for target in range(source, layers):
            rows = jnp.concatenate([own[target], errors_got[target]], 0)
            total = lax.dot_general(rows, values, contract, preferred_element_type=F32)
            out[block_index(source, target, layers)] = total.astype(BF)


def make_paired(n_tok):
    places = [(z, y, x, c) for z in range(n_tok) for y in range(2) for x in range(n_tok // 2) for c in range(2)]

    def swap(value, where):
        pairs = []
        for i, (z, y, x, c) in enumerate(places):
            to = where(z, y, x, c, c == z % 2)
            if to is not None:
                pairs.append((i, places.index(to)))
        return lax.ppermute(value, AXES, pairs)

    def over_c(value):
        return swap(value, lambda z, y, x, c, home: (z, y, x, 1 - c))

    def over_x(value):
        return swap(value, lambda z, y, x, c, home: (z, y, 1 - x, c))

    def over_y(value):
        return swap(value, lambda z, y, x, c, home: (z, 1 - y, x, c))

    def over_z2_z1(value):
        return swap(value, lambda z, y, x, c, home: (z ^ 2, y, x, c) if home else (z ^ 1, y, x, 1 - c))


    def away_over_y(value):
        return swap(value, lambda z, y, x, c, home: (z ^ 1, y, x, 1 - c) if home else (z, 1 - y, x, c))

    def to_home_over_y(value):
        return swap(value, lambda z, y, x, c, home: (z, y if home else 1 - y, x, 1 - c))

    def to_away_over_z1(value):
        return swap(value, lambda z, y, x, c, home: (z ^ 1, y, x, c) if home else (z, y, x, 1 - c))

    def away_over_z3(value):
        return swap(value, lambda z, y, x, c, home: (z, 1 - y, x, c) if home else (z ^ 3, y, x, 1 - c))

    def gather(own):
        r1 = over_z2_z1(own)
        beside = to_home_over_y(own)
        third = to_away_over_z1(r1)
        r3 = over_y(r1)
        third, beside = lax.optimization_barrier((third, beside))
        return own, beside, third, away_over_y(third), r1, r3

    def reduce(q0, q1, q2, q3, home):
        near = q0 + over_y(q1).astype(F32)
        third = away_over_z3(near.astype(BF))
        got = over_z2_z1((q2 + over_y(q3).astype(F32)).astype(BF))
        return jnp.where(home, near, third.astype(F32)) + got.astype(F32)

    def local(inputs, targets, enc_weight, enc_bias, dec_weight, counts):
        rows, layers, width = inputs.shape
        latent_width = enc_weight.shape[2]
        both = 2 * width
        held = rows * n_tok
        lat, tok = lax.axis_index("lat"), lax.axis_index("tok")
        z, y, x, c = lat // 2, lat % 2, tok // 2, tok % 2
        home = z % 2 == c
        near = jnp.where(home, z, z ^ 3) // 2 == x
        info = jnp.stack([home, c, near]).astype(jnp.int32)
        dec_t = jnp.swapaxes(dec_weight, 1, 2)
        blocks = dec_t.shape[0]
        own_in, own_want = jnp.swapaxes(inputs, 0, 1), jnp.swapaxes(targets, 0, 1)

        def spread(own, first):
            rest = jnp.zeros_like(own)
            return jnp.where(first, jnp.concatenate([own, rest], 2), jnp.concatenate([rest, own], 2))

        def join(own, other):
            own = lax.optimization_barrier(spread(own, c == 0))
            left = lax.broadcasted_iota(jnp.int32, own.shape, 2) < width
            return jnp.where(left == (c == 0), own, spread(other, c != 0))

        block = join(own_in, over_c(own_in))
        block, enc_weight, dec_t, own_want = lax.optimization_barrier((block, enc_weight, dec_t, own_want))
        arrived = gather(block)
        (enc_all,) = fused(stack_kernel, [((layers, both, latent_width), BF)], info, enc_weight, over_c(enc_weight))
        (dec_all,) = fused(stack_kernel, [((blocks, both, latent_width), BF)], info, dec_t, over_c(dec_t))
        wanted = join(own_want, over_c(own_want))

        cuts = (0, layers - 1, layers)
        encoded = []
        for lo, hi in zip(cuts, cuts[1:]):
            tile = (hi - lo, held, latent_width)
            part, sent = fused(
                functools.partial(encode_kernel, lo),
                [(tile, F32), (tile, BF)],
                info,
                *arrived,
                enc_all,
                scratch=[((hi - lo, held, both), BF)],
            )
            encoded.append((part, over_x(sent)))
            arrived, part = lax.optimization_barrier((arrived, part))
            encoded[-1] = (part, encoded[-1][1])
        decoded = []
        for (lo, hi), (part, got) in zip(zip(cuts, cuts[1:]), encoded):
            piece = (hi, rows, both)
            decoded = fused(
                functools.partial(decode_kernel, lo, layers),
                [((hi, held, latent_width), BF), (piece, F32), (piece, F32), (piece, BF), (piece, BF)],
                counts[:, 0],
                part,
                got,
                enc_bias,
                dec_all,
                *decoded,
            )
        latents, q0, q2, q1, q3 = decoded
        mine = reduce(q0, q1, q2, q3, home)
        full = mine + over_c(mine)
        errors = (full - wanted.astype(F32)).astype(BF)
        recon = jnp.where(c == 0, full[:, :, :width], full[:, :, width:]).astype(BF)
        arrived = gather(errors)
        latents_got = over_c(latents)
        arrived, recon, latents_got = lax.optimization_barrier((arrived, recon, latents_got))
        narrow = (layers, held // 2, latent_width)
        kept, sent, all_errors = fused(
            backward_kernel,
            [(narrow, F32), (narrow, BF), ((layers, held, both), BF)],
            info,
            *arrived,
            dec_all,
        )
        got = over_x(sent)
        other = jnp.where(c == 0, all_errors[:, :, width:], all_errors[:, :, :width])
        (grads,) = fused(
            weight_grad_kernel,
            [((blocks, width, latent_width), BF)],
            info,
            all_errors,
            over_c(other),
            latents,
            latents_got,
            scratch=[((layers, held, width), BF)],
        )
        got, grads = lax.optimization_barrier((got, grads))
        total = kept + got.astype(F32)
        flipped = jnp.concatenate([total[:, rows:], total[:, :rows]], 1)
        live = (lax.broadcasted_iota(jnp.int32, (layers, latent_width), 1) < counts)[:, None, :]
        latent_grad = jnp.where(live, jnp.where(y == 0, total, flipped), 0.0).astype(BF)
        return jnp.swapaxes(recon, 0, 1), jnp.swapaxes(grads, 1, 2), jnp.swapaxes(latent_grad, 0, 1)

    return local


def general(inputs, targets, enc_weight, enc_bias, dec_weight, counts):
    layers = inputs.shape[1]
    width = enc_weight.shape[2]
    live = (lax.broadcasted_iota(jnp.int32, (layers, width), 1) < counts)[None]
    gathered = lax.all_gather(inputs, "lat", axis=0, tiled=True)
    part = jnp.einsum("tld,ldk->tlk", gathered, enc_weight, preferred_element_type=F32)
    preact = lax.psum(part, "tok") + enc_bias[None]
    latents = jnp.where(live, jnp.maximum(preact, 0.0), 0.0).astype(BF)
    recons = []
    for target in range(layers):
        recons.append(
            sum(
                jnp.dot(
                    latents[:, source],
                    dec_weight[block_index(source, target, layers)],
                    preferred_element_type=F32,
                )
                for source in range(target + 1)
            )
        )
    full = lax.psum_scatter(jnp.stack(recons, 1), "lat", scatter_dimension=0, tiled=True)
    own_errors = (full - targets.astype(F32)).astype(BF)
    errors = lax.all_gather(own_errors, "lat", axis=0, tiled=True)
    grads, sums = [], []
    for source in range(layers):
        total = 0.0
        for target in range(source, layers):
            weight = dec_weight[block_index(source, target, layers)]
            total = total + lax.dot_general(
                errors[:, target], weight, (((1,), (1,)), ((), ())), preferred_element_type=F32
            )
            grads.append(
                lax.dot_general(
                    latents[:, source],
                    errors[:, target],
                    (((0,), (0,)), ((), ())),
                    preferred_element_type=F32,
                ).astype(BF)
            )
        sums.append(total)
    latent_sum = lax.psum_scatter(jnp.stack(sums, 1), "tok", scatter_dimension=0, tiled=True)
    latent_grad = jnp.where(live, latent_sum, 0.0).astype(BF)
    return full.astype(BF), jnp.stack(grads, 0), latent_grad


def solution(mesh):
    n_lat, n_tok = mesh.shape["lat"], mesh.shape["tok"]
    in_specs = (
        P("lat", None, "tok"),
        P("lat", None, "tok"),
        P(None, "tok", "lat"),
        P(None, "lat"),
        P(None, "lat", "tok"),
        P(None, "lat"),
    )
    out_specs = (P("lat", None, "tok"), P(None, "lat", "tok"), P("tok", None, "lat"))
    paired = n_lat == 2 * n_tok and n_tok == 4
    local = make_paired(n_tok) if paired else general
    return jax.shard_map(local, mesh=mesh, in_specs=in_specs, out_specs=out_specs, check_vma=False)
```

```python
import functools

import jax
import jax.numpy as jnp
from jax import lax
from jax.experimental import pallas as pl
from jax.experimental.pallas import tpu as pltpu
from jax.sharding import PartitionSpec as P

BF = jnp.bfloat16
F32 = jnp.float32
AXES = ("lat", "tok")


def block_index(source, target, layers):
    return source * layers - source * (source - 1) // 2 + (target - source)


def fused(body, outs, *args, scratch=(), scalars=1):
    specs = [pl.BlockSpec(memory_space=pltpu.SMEM)] * scalars
    specs += [pl.BlockSpec(memory_space=pltpu.VMEM)] * (len(args) - scalars)
    out_shape = [jax.ShapeDtypeStruct(s, d) for s, d in outs]
    return pl.pallas_call(
        body,
        out_shape=out_shape,
        in_specs=specs,
        out_specs=[pl.BlockSpec(memory_space=pltpu.VMEM)] * len(outs),
        scratch_shapes=[pltpu.VMEM(s, d) for s, d in scratch],
        compiler_params=pltpu.CompilerParams(vmem_limit_bytes=40 * 2**20),
    )(*args)


HOME, CORE, NEAR = 0, 1, 2


def stack_kernel(info, own, other, out):
    rows = own.shape[1]
    core = info[CORE]
    out[:, pl.ds(pl.multiple_of(core * rows, rows), rows), :] = own[...]
    out[:, pl.ds(pl.multiple_of((1 - core) * rows, rows), rows), :] = other[...]


def place(info, own, beside, third, fourth, r1, r3, out):
    rows = own.shape[1]

    @pl.when(info[HOME] != 0)
    def _():
        out[:, :rows, :] = own[...]
        out[:, 2 * rows : 3 * rows, :] = beside[...]

    @pl.when(info[HOME] == 0)
    def _():
        out[:, :rows, :] = third[...]
        out[:, 2 * rows : 3 * rows, :] = fourth[...]

    out[:, rows : 2 * rows, :] = r1[...]
    out[:, 3 * rows :, :] = r3[...]


def encode_kernel(info, at_home, away, second, weight, part, sent, held):
    rows = second.shape[1]

    @pl.when(info[HOME] != 0)
    def _():
        held[:, :rows, :] = at_home[...]

    @pl.when(info[HOME] == 0)
    def _():
        held[:, :rows, :] = away[...]

    held[:, rows:, :] = second[...]
    for layer in range(part.shape[0]):
        value = jnp.dot(held[layer], weight[layer], preferred_element_type=F32)
        part[layer] = value
        sent[layer] = value.astype(BF)


def decode_kernel(counts, part, got, bias, weight, latents, first, second):
    layers, held, width = part.shape
    rows = first.shape[1]
    for layer in range(layers):
        live = lax.broadcasted_iota(jnp.int32, (held, width), 1) < counts[layer]
        pre = part[layer] + got[layer].astype(F32) + bias[layer : layer + 1, :]
        latents[layer] = jnp.where(live, jnp.maximum(pre, 0.0), 0.0).astype(BF)
    for target in range(layers):
        total = None
        for source in range(target + 1):
            value = lax.dot_general(
                latents[source],
                weight[block_index(source, target, layers)],
                (((1,), (1,)), ((), ())),
                preferred_element_type=F32,
            )
            total = value if total is None else total + value
        first[target] = total[:rows].astype(first.dtype)
        second[target] = total[rows:].astype(second.dtype)


def backward_kernel(info, own, beside, third, fourth, r1, r3, weight, kept, sent, held):
    place(info, own, beside, third, fourth, r1, r3, held)
    layers, rows = kept.shape[0], own.shape[1]
    for source in range(layers):
        total = None
        for target in range(source, layers):
            value = jnp.dot(
                held[target], weight[block_index(source, target, layers)], preferred_element_type=F32
            )
            total = value if total is None else total + value
        stays = info[NEAR] != 0
        for i in range(2):
            to = slice(i * rows, (i + 1) * rows)
            one, two = total[2 * i * rows : (2 * i + 1) * rows], total[(2 * i + 1) * rows : (2 * i + 2) * rows]
            kept[source, to] = jnp.where(stays, one, two)
            sent[source, to] = jnp.where(stays, two, one).astype(BF)


def weight_grad_kernel(info, held, errors_got, latents, latents_got, out, own, blocks, sems):
    layers = latents.shape[0]
    width = errors_got.shape[2]

    @pl.when(info[CORE] == 0)
    def _():
        own[...] = held[:, :, :width]

    @pl.when(info[CORE] != 0)
    def _():
        own[...] = held[:, :, width:]

    copies = []
    for target in range(layers):
        rows = jnp.concatenate([own[target], errors_got[target]], 0)
        for source in range(target + 1):
            values = jnp.concatenate([latents[source], latents_got[source]], 0)
            total = lax.dot_general(rows, values, (((0,), (0,)), ((), ())), preferred_element_type=F32)
            at = block_index(source, target, layers)
            blocks[at] = total.astype(BF)
            copies.append(pltpu.make_async_copy(blocks.at[at], out.at[at], sems.at[at]))
            copies[-1].start()
    for copy in copies:
        copy.wait()


def make_paired(n_tok):
    places = [(z, y, x, c) for z in range(n_tok) for y in range(2) for x in range(n_tok // 2) for c in range(2)]

    def swap(value, where):
        pairs = []
        for i, (z, y, x, c) in enumerate(places):
            to = where(z, y, x, c, c == z % 2)
            if to is not None:
                pairs.append((i, places.index(to)))
        return lax.ppermute(value, AXES, pairs)

    def over_c(value):
        return swap(value, lambda z, y, x, c, home: (z, y, x, 1 - c))

    def over_x(value):
        return swap(value, lambda z, y, x, c, home: (z, y, 1 - x, c))

    def over_y(value):
        return swap(value, lambda z, y, x, c, home: (z, 1 - y, x, c))

    def over_z2_z1(value):
        return swap(value, lambda z, y, x, c, home: (z ^ 2, y, x, c) if home else (z ^ 1, y, x, 1 - c))


    def away_over_y(value):
        return swap(value, lambda z, y, x, c, home: (z ^ 1, y, x, 1 - c) if home else (z, 1 - y, x, c))

    def to_home_over_y(value):
        return swap(value, lambda z, y, x, c, home: (z, y if home else 1 - y, x, 1 - c))

    def to_away_over_z1(value):
        return swap(value, lambda z, y, x, c, home: (z ^ 1, y, x, c) if home else (z, y, x, 1 - c))

    def away_over_z3(value):
        return swap(value, lambda z, y, x, c, home: (z, 1 - y, x, c) if home else (z ^ 3, y, x, 1 - c))

    def gather(own, ready=None):
        r1 = over_z2_z1(own)
        beside = to_home_over_y(own)
        if ready is not None:
            r1, ready = lax.optimization_barrier((r1, ready))
        third = to_away_over_z1(r1)
        r3 = over_y(r1)
        third, beside = lax.optimization_barrier((third, beside))
        blocks = own, beside, third, away_over_y(third), r1, r3
        return blocks if ready is None else blocks + (ready,)

    def reduce(q0, q1, q2, q3, home):
        near = q0 + over_y(q1).astype(F32)
        third = away_over_z3(near.astype(BF))
        got = over_z2_z1((q2 + over_y(q3).astype(F32)).astype(BF))
        return jnp.where(home, near, third.astype(F32)) + got.astype(F32)

    def local(inputs, targets, enc_weight, enc_bias, dec_weight, counts):
        rows, layers, width = inputs.shape
        latent_width = enc_weight.shape[2]
        both = 2 * width
        held = rows * n_tok
        lat, tok = lax.axis_index("lat"), lax.axis_index("tok")
        z, y, x, c = lat // 2, lat % 2, tok // 2, tok % 2
        home = z % 2 == c
        near = jnp.where(home, z, z ^ 3) // 2 == x
        info = jnp.stack([home, c, near]).astype(jnp.int32)
        dec_t = jnp.swapaxes(dec_weight, 1, 2)
        blocks = dec_t.shape[0]
        own_in, own_want = jnp.swapaxes(inputs, 0, 1), jnp.swapaxes(targets, 0, 1)

        def spread(own, first):
            rest = jnp.zeros_like(own)
            return jnp.where(first, jnp.concatenate([own, rest], 2), jnp.concatenate([rest, own], 2))

        def join(own, other):
            own = lax.optimization_barrier(spread(own, c == 0))
            left = lax.broadcasted_iota(jnp.int32, own.shape, 2) < width
            return jnp.where(left == (c == 0), own, spread(other, c != 0))

        block = join(own_in, over_c(own_in))
        block, enc_weight, dec_t, own_want = lax.optimization_barrier((block, enc_weight, dec_t, own_want))
        (enc_all,) = fused(stack_kernel, [((layers, both, latent_width), BF)], info, enc_weight, over_c(enc_weight))
        *arrived, enc_all = gather(block, enc_all)
        (dec_all,) = fused(stack_kernel, [((blocks, both, latent_width), BF)], info, dec_t, over_c(dec_t))
        wanted = join(own_want, over_c(own_want))

        own_block, beside, third, fourth, r1, r3 = arrived
        tile = (layers, 2 * rows, latent_width)
        piece = (layers, rows, both)

        def encode(*parts):
            return fused(
                encode_kernel,
                [(tile, F32), (tile, BF)],
                info,
                *parts,
                enc_all,
                scratch=[((layers, 2 * rows, both), BF)],
            )

        def decode(part, got, kind):
            outs = [(tile, BF), (piece, kind), (piece, kind)]
            return fused(decode_kernel, outs, counts[:, 0], part, got, enc_bias, dec_all)

        part, sent = encode(own_block, third, r1)
        got = over_x(sent)
        beside, fourth, r3, part = lax.optimization_barrier((beside, fourth, r3, part))
        late_part, late_sent = encode(beside, fourth, r3)
        late_got = over_x(late_sent)
        part, late_part = lax.optimization_barrier((part, late_part))
        early, q0, q2 = decode(part, got, F32)
        late_part, late_got, early = lax.optimization_barrier((late_part, late_got, early))
        late, q1, q3 = decode(late_part, late_got, BF)
        latents = jnp.concatenate([early, late], 1)
        mine = reduce(q0, q1, q2, q3, home)
        full = mine + over_c(mine)
        errors = (full - wanted.astype(F32)).astype(BF)
        recon = jnp.where(c == 0, full[:, :, :width], full[:, :, width:]).astype(BF)
        arrived = gather(errors)
        latents_got = over_c(latents)
        arrived, recon, latents_got = lax.optimization_barrier((arrived, recon, latents_got))
        narrow = (layers, held // 2, latent_width)
        kept, sent, all_errors = fused(
            backward_kernel,
            [(narrow, F32), (narrow, BF), ((layers, held, both), BF)],
            info,
            *arrived,
            dec_all,
        )
        got = over_x(sent)
        other = jnp.where(c == 0, all_errors[:, :, width:], all_errors[:, :, :width])
        vmem = pl.BlockSpec(memory_space=pltpu.VMEM)
        shape = (blocks, width, latent_width)
        grads = pl.pallas_call(
            weight_grad_kernel,
            out_shape=jax.ShapeDtypeStruct(shape, BF),
            in_specs=[pl.BlockSpec(memory_space=pltpu.SMEM)] + [vmem] * 4,
            out_specs=pl.BlockSpec(memory_space=pl.ANY),
            scratch_shapes=[
                pltpu.VMEM((layers, held, width), BF),
                pltpu.VMEM(shape, BF),
                pltpu.SemaphoreType.DMA((blocks,)),
            ],
            compiler_params=pltpu.CompilerParams(vmem_limit_bytes=40 * 2**20),
        )(info, all_errors, over_c(other), latents, latents_got)
        got, grads = lax.optimization_barrier((got, grads))
        total = kept + got.astype(F32)
        flipped = jnp.concatenate([total[:, rows:], total[:, :rows]], 1)
        live = (lax.broadcasted_iota(jnp.int32, (layers, latent_width), 1) < counts)[:, None, :]
        latent_grad = jnp.where(live, jnp.where(y == 0, total, flipped), 0.0).astype(BF)
        return jnp.swapaxes(recon, 0, 1), jnp.swapaxes(grads, 1, 2), jnp.swapaxes(latent_grad, 0, 1)

    return local


def general(inputs, targets, enc_weight, enc_bias, dec_weight, counts):
    layers = inputs.shape[1]
    width = enc_weight.shape[2]
    live = (lax.broadcasted_iota(jnp.int32, (layers, width), 1) < counts)[None]
    gathered = lax.all_gather(inputs, "lat", axis=0, tiled=True)
    part = jnp.einsum("tld,ldk->tlk", gathered, enc_weight, preferred_element_type=F32)
    preact = lax.psum(part, "tok") + enc_bias[None]
    latents = jnp.where(live, jnp.maximum(preact, 0.0), 0.0).astype(BF)
    recons = []
    for target in range(layers):
        recons.append(
            sum(
                jnp.dot(
                    latents[:, source],
                    dec_weight[block_index(source, target, layers)],
                    preferred_element_type=F32,
                )
                for source in range(target + 1)
            )
        )
    full = lax.psum_scatter(jnp.stack(recons, 1), "lat", scatter_dimension=0, tiled=True)
    own_errors = (full - targets.astype(F32)).astype(BF)
    errors = lax.all_gather(own_errors, "lat", axis=0, tiled=True)
    grads, sums = [], []
    for source in range(layers):
        total = 0.0
        for target in range(source, layers):
            weight = dec_weight[block_index(source, target, layers)]
            total = total + lax.dot_general(
                errors[:, target], weight, (((1,), (1,)), ((), ())), preferred_element_type=F32
            )
            grads.append(
                lax.dot_general(
                    latents[:, source],
                    errors[:, target],
                    (((0,), (0,)), ((), ())),
                    preferred_element_type=F32,
                ).astype(BF)
            )
        sums.append(total)
    latent_sum = lax.psum_scatter(jnp.stack(sums, 1), "tok", scatter_dimension=0, tiled=True)
    latent_grad = jnp.where(live, latent_sum, 0.0).astype(BF)
    return full.astype(BF), jnp.stack(grads, 0), latent_grad


def solution(mesh):
    n_lat, n_tok = mesh.shape["lat"], mesh.shape["tok"]
    in_specs = (
        P("lat", None, "tok"),
        P("lat", None, "tok"),
        P(None, "tok", "lat"),
        P(None, "lat"),
        P(None, "lat", "tok"),
        P(None, "lat"),
    )
    out_specs = (P("lat", None, "tok"), P(None, "lat", "tok"), P("tok", None, "lat"))
    paired = n_lat == 2 * n_tok and n_tok == 4
    local = make_paired(n_tok) if paired else general
    return jax.shard_map(local, mesh=mesh, in_specs=in_specs, out_specs=out_specs, check_vma=False)
```

```python
import functools

import jax
import jax.numpy as jnp
from jax import lax
from jax.experimental import pallas as pl
from jax.experimental.pallas import tpu as pltpu
from jax.sharding import PartitionSpec as P

BF = jnp.bfloat16
F32 = jnp.float32
AXES = ("lat", "tok")


def block_index(source, target, layers):
    return source * layers - source * (source - 1) // 2 + (target - source)


def fused(body, outs, *args, scratch=(), scalars=1):
    specs = [pl.BlockSpec(memory_space=pltpu.SMEM)] * scalars
    specs += [pl.BlockSpec(memory_space=pltpu.VMEM)] * (len(args) - scalars)
    out_shape = [jax.ShapeDtypeStruct(s, d) for s, d in outs]
    return pl.pallas_call(
        body,
        out_shape=out_shape,
        in_specs=specs,
        out_specs=[pl.BlockSpec(memory_space=pltpu.VMEM)] * len(outs),
        scratch_shapes=[pltpu.VMEM(s, d) for s, d in scratch],
        compiler_params=pltpu.CompilerParams(vmem_limit_bytes=40 * 2**20),
    )(*args)


HOME, CORE, NEAR = 0, 1, 2


def stack_kernel(info, own, other, out):
    rows = own.shape[1]
    core = info[CORE]
    out[:, pl.ds(pl.multiple_of(core * rows, rows), rows), :] = own[...]
    out[:, pl.ds(pl.multiple_of((1 - core) * rows, rows), rows), :] = other[...]


def place(info, own, beside, third, fourth, r1, r3, out):
    rows = own.shape[1]

    @pl.when(info[HOME] != 0)
    def _():
        out[:, :rows, :] = own[...]
        out[:, 2 * rows : 3 * rows, :] = beside[...]

    @pl.when(info[HOME] == 0)
    def _():
        out[:, :rows, :] = third[...]
        out[:, 2 * rows : 3 * rows, :] = fourth[...]

    out[:, rows : 2 * rows, :] = r1[...]
    out[:, 3 * rows :, :] = r3[...]


def encode_kernel(info, at_home, away, second, weight, part, sent, held):
    rows = second.shape[1]

    @pl.when(info[HOME] != 0)
    def _():
        held[:, :rows, :] = at_home[...]

    @pl.when(info[HOME] == 0)
    def _():
        held[:, :rows, :] = away[...]

    held[:, rows:, :] = second[...]
    for layer in range(part.shape[0]):
        value = jnp.dot(held[layer], weight[layer], preferred_element_type=F32)
        part[layer] = value
        sent[layer] = value.astype(BF)


def decode_kernel(counts, part, got, bias, weight, latents, first, second):
    layers, held, width = part.shape
    rows = first.shape[1]
    for layer in range(layers):
        live = lax.broadcasted_iota(jnp.int32, (held, width), 1) < counts[layer]
        pre = part[layer] + got[layer].astype(F32) + bias[layer : layer + 1, :]
        latents[layer] = jnp.where(live, jnp.maximum(pre, 0.0), 0.0).astype(BF)
    for target in range(layers):
        total = None
        for source in range(target + 1):
            value = lax.dot_general(
                latents[source],
                weight[block_index(source, target, layers)],
                (((1,), (1,)), ((), ())),
                preferred_element_type=F32,
            )
            total = value if total is None else total + value
        first[target] = total[:rows].astype(first.dtype)
        second[target] = total[rows:].astype(second.dtype)


def backward_kernel(info, own, beside, third, fourth, r1, r3, weight, kept, sent, held):
    place(info, own, beside, third, fourth, r1, r3, held)
    layers, rows = kept.shape[0], own.shape[1]
    for source in range(layers):
        total = None
        for target in range(source, layers):
            value = jnp.dot(
                held[target], weight[block_index(source, target, layers)], preferred_element_type=F32
            )
            total = value if total is None else total + value
        stays = info[NEAR] != 0
        for i in range(2):
            to = slice(i * rows, (i + 1) * rows)
            one, two = total[2 * i * rows : (2 * i + 1) * rows], total[(2 * i + 1) * rows : (2 * i + 2) * rows]
            kept[source, to] = jnp.where(stays, one, two)
            sent[source, to] = jnp.where(stays, two, one).astype(BF)


def weight_grad_kernel(info, held, errors_got, latents, latents_got, out, own, blocks, sems):
    layers = latents.shape[0]
    width = errors_got.shape[2]

    @pl.when(info[CORE] == 0)
    def _():
        own[...] = held[:, :, :width]

    @pl.when(info[CORE] != 0)
    def _():
        own[...] = held[:, :, width:]

    copies = []
    for target in range(layers):
        across = jnp.concatenate([own[target], errors_got[target]], 0).T
        for source in range(target + 1):
            values = jnp.concatenate([latents[source], latents_got[source]], 0)
            total = jnp.dot(across, values, preferred_element_type=F32)
            at = block_index(source, target, layers)
            blocks[at] = total.astype(BF)
            copies.append(pltpu.make_async_copy(blocks.at[at], out.at[at], sems.at[at]))
            copies[-1].start()
    for copy in copies:
        copy.wait()


def make_paired(n_tok):
    places = [(z, y, x, c) for z in range(n_tok) for y in range(2) for x in range(n_tok // 2) for c in range(2)]

    def swap(value, where):
        pairs = []
        for i, (z, y, x, c) in enumerate(places):
            to = where(z, y, x, c, c == z % 2)
            if to is not None:
                pairs.append((i, places.index(to)))
        return lax.ppermute(value, AXES, pairs)

    def over_c(value):
        return swap(value, lambda z, y, x, c, home: (z, y, x, 1 - c))

    def over_x(value):
        return swap(value, lambda z, y, x, c, home: (z, y, 1 - x, c))

    def over_y(value):
        return swap(value, lambda z, y, x, c, home: (z, 1 - y, x, c))

    def over_z2_z1(value):
        return swap(value, lambda z, y, x, c, home: (z ^ 2, y, x, c) if home else (z ^ 1, y, x, 1 - c))


    def away_over_y(value):
        return swap(value, lambda z, y, x, c, home: (z ^ 1, y, x, 1 - c) if home else (z, 1 - y, x, c))

    def to_home_over_y(value):
        return swap(value, lambda z, y, x, c, home: (z, y if home else 1 - y, x, 1 - c))

    def to_away_over_z1(value):
        return swap(value, lambda z, y, x, c, home: (z ^ 1, y, x, c) if home else (z, y, x, 1 - c))

    def away_over_z3(value):
        return swap(value, lambda z, y, x, c, home: (z, 1 - y, x, c) if home else (z ^ 3, y, x, 1 - c))

    def gather(own, ready=None):
        r1 = over_z2_z1(own)
        beside = to_home_over_y(own)
        if ready is not None:
            r1, ready = lax.optimization_barrier((r1, ready))
        third = to_away_over_z1(r1)
        r3 = over_y(r1)
        third, beside = lax.optimization_barrier((third, beside))
        blocks = own, beside, third, away_over_y(third), r1, r3
        return blocks if ready is None else blocks + (ready,)

    def reduce(q0, q1, q2, q3, home):
        near = q0 + over_y(q1).astype(F32)
        third = away_over_z3(near.astype(BF))
        got = over_z2_z1((q2 + over_y(q3).astype(F32)).astype(BF))
        return jnp.where(home, near, third.astype(F32)) + got.astype(F32)

    def local(inputs, targets, enc_weight, enc_bias, dec_weight, counts):
        rows, layers, width = inputs.shape
        latent_width = enc_weight.shape[2]
        both = 2 * width
        held = rows * n_tok
        lat, tok = lax.axis_index("lat"), lax.axis_index("tok")
        z, y, x, c = lat // 2, lat % 2, tok // 2, tok % 2
        home = z % 2 == c
        near = jnp.where(home, z, z ^ 3) // 2 == x
        info = jnp.stack([home, c, near]).astype(jnp.int32)
        dec_t = jnp.swapaxes(dec_weight, 1, 2)
        blocks = dec_t.shape[0]
        own_in, own_want = jnp.swapaxes(inputs, 0, 1), jnp.swapaxes(targets, 0, 1)

        def spread(own, first):
            rest = jnp.zeros_like(own)
            return jnp.where(first, jnp.concatenate([own, rest], 2), jnp.concatenate([rest, own], 2))

        def join(own, other):
            own = lax.optimization_barrier(spread(own, c == 0))
            left = lax.broadcasted_iota(jnp.int32, own.shape, 2) < width
            return jnp.where(left == (c == 0), own, spread(other, c != 0))

        block = join(own_in, over_c(own_in))
        block, enc_weight, dec_t, own_want = lax.optimization_barrier((block, enc_weight, dec_t, own_want))
        (enc_all,) = fused(stack_kernel, [((layers, both, latent_width), BF)], info, enc_weight, over_c(enc_weight))
        *arrived, enc_all = gather(block, enc_all)
        (dec_all,) = fused(stack_kernel, [((blocks, both, latent_width), BF)], info, dec_t, over_c(dec_t))
        wanted = join(own_want, over_c(own_want))

        own_block, beside, third, fourth, r1, r3 = arrived
        tile = (layers, 2 * rows, latent_width)
        piece = (layers, rows, both)

        def encode(*parts):
            return fused(
                encode_kernel,
                [(tile, F32), (tile, BF)],
                info,
                *parts,
                enc_all,
                scratch=[((layers, 2 * rows, both), BF)],
            )

        def decode(part, got, kind):
            outs = [(tile, BF), (piece, kind), (piece, kind)]
            return fused(decode_kernel, outs, counts[:, 0], part, got, enc_bias, dec_all)

        part, sent = encode(own_block, third, r1)
        got = over_x(sent)
        beside, fourth, r3, part = lax.optimization_barrier((beside, fourth, r3, part))
        late_part, late_sent = encode(beside, fourth, r3)
        late_got = over_x(late_sent)
        part, late_part = lax.optimization_barrier((part, late_part))
        part, wanted = lax.optimization_barrier((part, wanted))
        early, q0, q2 = decode(part, got, F32)
        late_part, late_got, early = lax.optimization_barrier((late_part, late_got, early))
        late, q1, q3 = decode(late_part, late_got, BF)
        latents = jnp.concatenate([early, late], 1)
        mine = reduce(q0, q1, q2, q3, home)
        full = mine + over_c(mine)
        errors = (full - wanted.astype(F32)).astype(BF)
        recon = jnp.where(c == 0, full[:, :, :width], full[:, :, width:]).astype(BF)
        arrived = gather(errors)
        latents_got = over_c(latents)
        arrived, recon, latents_got = lax.optimization_barrier((arrived, recon, latents_got))
        narrow = (layers, held // 2, latent_width)
        kept, sent, all_errors = fused(
            backward_kernel,
            [(narrow, F32), (narrow, BF), ((layers, held, both), BF)],
            info,
            *arrived,
            dec_all,
        )
        got = over_x(sent)
        other = jnp.where(c == 0, all_errors[:, :, width:], all_errors[:, :, :width])
        vmem = pl.BlockSpec(memory_space=pltpu.VMEM)
        shape = (blocks, width, latent_width)
        grads = pl.pallas_call(
            weight_grad_kernel,
            out_shape=jax.ShapeDtypeStruct(shape, BF),
            in_specs=[pl.BlockSpec(memory_space=pltpu.SMEM)] + [vmem] * 4,
            out_specs=pl.BlockSpec(memory_space=pl.ANY),
            scratch_shapes=[
                pltpu.VMEM((layers, held, width), BF),
                pltpu.VMEM(shape, BF),
                pltpu.SemaphoreType.DMA((blocks,)),
            ],
            compiler_params=pltpu.CompilerParams(vmem_limit_bytes=40 * 2**20),
        )(info, all_errors, over_c(other), latents, latents_got)
        got, grads = lax.optimization_barrier((got, grads))
        total = kept + got.astype(F32)
        flipped = jnp.concatenate([total[:, rows:], total[:, :rows]], 1)
        live = (lax.broadcasted_iota(jnp.int32, (layers, latent_width), 1) < counts)[:, None, :]
        latent_grad = jnp.where(live, jnp.where(y == 0, total, flipped), 0.0).astype(BF)
        return jnp.swapaxes(recon, 0, 1), jnp.swapaxes(grads, 1, 2), jnp.swapaxes(latent_grad, 0, 1)

    return local


def general(inputs, targets, enc_weight, enc_bias, dec_weight, counts):
    layers = inputs.shape[1]
    width = enc_weight.shape[2]
    live = (lax.broadcasted_iota(jnp.int32, (layers, width), 1) < counts)[None]
    gathered = lax.all_gather(inputs, "lat", axis=0, tiled=True)
    part = jnp.einsum("tld,ldk->tlk", gathered, enc_weight, preferred_element_type=F32)
    preact = lax.psum(part, "tok") + enc_bias[None]
    latents = jnp.where(live, jnp.maximum(preact, 0.0), 0.0).astype(BF)
    recons = []
    for target in range(layers):
        recons.append(
            sum(
                jnp.dot(
                    latents[:, source],
                    dec_weight[block_index(source, target, layers)],
                    preferred_element_type=F32,
                )
                for source in range(target + 1)
            )
        )
    full = lax.psum_scatter(jnp.stack(recons, 1), "lat", scatter_dimension=0, tiled=True)
    own_errors = (full - targets.astype(F32)).astype(BF)
    errors = lax.all_gather(own_errors, "lat", axis=0, tiled=True)
    grads, sums = [], []
    for source in range(layers):
        total = 0.0
        for target in range(source, layers):
            weight = dec_weight[block_index(source, target, layers)]
            total = total + lax.dot_general(
                errors[:, target], weight, (((1,), (1,)), ((), ())), preferred_element_type=F32
            )
            grads.append(
                lax.dot_general(
                    latents[:, source],
                    errors[:, target],
                    (((0,), (0,)), ((), ())),
                    preferred_element_type=F32,
                ).astype(BF)
            )
        sums.append(total)
    latent_sum = lax.psum_scatter(jnp.stack(sums, 1), "tok", scatter_dimension=0, tiled=True)
    latent_grad = jnp.where(live, latent_sum, 0.0).astype(BF)
    return full.astype(BF), jnp.stack(grads, 0), latent_grad


def solution(mesh):
    n_lat, n_tok = mesh.shape["lat"], mesh.shape["tok"]
    in_specs = (
        P("lat", None, "tok"),
        P("lat", None, "tok"),
        P(None, "tok", "lat"),
        P(None, "lat"),
        P(None, "lat", "tok"),
        P(None, "lat"),
    )
    out_specs = (P("lat", None, "tok"), P(None, "lat", "tok"), P("tok", None, "lat"))
    paired = n_lat == 2 * n_tok and n_tok == 4
    local = make_paired(n_tok) if paired else general
    return jax.shard_map(local, mesh=mesh, in_specs=in_specs, out_specs=out_specs, check_vma=False)
```
